256 devices in a mesh: group: 4 (over y), owner: 64 (over z, x, core).
Axes of the slice: x: 4, y: 4, z: 8, core: 2. Of those that a mesh axis runs over, the one named last changes fastest.
Arguments:
- field: float32 [64, 32768], P(None, ('group', 'owner')), may hold values from -6 to 6
- contrast: float32 [64, 32768], P(None, ('group', 'owner')), may hold values from 0.1 to 2
- incident: float32 [64, 32768], P(None, ('group', 'owner')), may hold values from -6 to 6
- near_lists: int32 [27, 32768], P(None, ('group', 'owner')), may hold values from -1 to 128, as said below
- far_lists: int32 [316, 37376], P(None, ('group', 'owner')), may hold values from -1 to 511, as said below
- near_mats: float32 [27, 64, 64], replicated, may hold values from -0.15625 to 0.15625
- far_mats: float32 [316, 49, 49], replicated, may hold values from -0.0625 to 0.0625
- up_mats: float32 [8, 49, 49], replicated, may hold values from -0.3125 to 0.3125
- down_mats: float32 [8, 49, 49], replicated, may hold values from -0.875 to 0.875
- moment_map: float32 [49, 64], replicated, may hold values from -0.75 to 0.75
- local_map: float32 [64, 49], replicated, may hold values from -0.5 to 0.5
Outputs:
- new_field: float32 [64, 32768], P(None, ('group', 'owner'))
The draws below stay inside these ranges and needn't reach their ends.
Inputs may be any that keep to these rules, and one draw needn't show every extreme that they name: -1 marks an empty slot; otherwise b + near_lists[k, b] - 64 is a leaf box, and slot 13 of every box holds 64. `far_lists`: -1 marks an empty slot; otherwise the entry names a box of the column's level as the steps say: below level 2 an entry of 0 to w_l, at level 2 any box of that level.
All inputs are finite; a program needn't handle non-finite values.
Results may differ from the reference program's by a relative error of at most 0.0003.
Values sent between devices are 32-bit elements; how exact they have to be, the bound alone decides.
A program may use at most 128 MiB of HBM per device.

```python
import math
import jax
import jax.numpy as jnp
import numpy as np
from jax import lax

CELLS = 64
TERMS = 49
NNEAR = 27
NFAR = 316
LOCAL = 2
TOPS = 2
BPD = 128
NEARW = 64
BOXDEV = 146
NBOX = 32768
FARCOLS = 37376
N_GROUP = 4
N_OWNER = 64


def draw_near_lists(key, part):
    key_shift, key_keep, key_load = jax.random.split(key, 3)
    devices = NBOX // BPD
    slots = jnp.arange(NNEAR, dtype=jnp.int32)[:, None]
    boxes = jnp.arange(NBOX, dtype=jnp.int32)[None, :]
    offset = jax.random.randint(key_shift, (NNEAR, NBOX), -NEARW, NEARW + 1)
    burden = jax.random.randint(key_load, (devices,), 2, 8)
    ceiling = jnp.repeat(burden, BPD)[None, :]
    kept = jax.random.randint(key_keep, (NNEAR, NBOX), 0, 8) < ceiling
    centre = slots == NNEAR // 2
    reach_top = (slots == 1) & (boxes == 0)
    offset = jnp.where(reach_top, NEARW, offset)
    kept = (kept | centre | reach_top) & jnp.logical_not((slots == 0) & (boxes == 0))
    partner = jnp.clip(boxes + jnp.where(centre, 0, offset), 0, NBOX - 1)
    value = partner - boxes + NEARW
    return jnp.where(kept, value, -1).astype(jnp.int32)


def draw_far_lists(key, part):
    spans = [TOPS * 8 ** (LOCAL - level) for level in range(LOCAL + 1)]
    devices = NBOX // BPD
    level_of = np.concatenate([np.full(span, level) for level, span in enumerate(spans)])
    inside = np.concatenate([np.arange(span) for span in spans])
    span_of = np.concatenate([np.full(span, span) for span in spans])
    device_of = np.repeat(np.arange(devices), BOXDEV)
    span_every = np.tile(span_of, devices)
    level_every = jnp.asarray(np.tile(level_of, devices), jnp.int32)[None, :]
    own_box = jnp.asarray(device_of * span_every + np.tile(inside, devices), jnp.int32)[None, :]
    level_count = jnp.asarray(span_every * devices, jnp.int32)[None, :]
    half_wide = jnp.asarray(span_every // 2, jnp.int32)[None, :]
    key_pick, key_keep, key_load = jax.random.split(key, 3)
    drawn = jax.random.randint(key_pick, (NFAR, FARCOLS), 0, 1 << 20)
    offset = drawn % (2 * half_wide + 1) - half_wide
    slots = jnp.arange(NFAR, dtype=jnp.int32)[:, None]
    columns = jnp.arange(FARCOLS, dtype=jnp.int32)[None, :]
    reach_close = (slots == 1) & (columns == 0)
    offset = jnp.where(reach_close, half_wide, offset)
    close_value = jnp.clip(own_box + offset, 0, level_count - 1) - own_box + half_wide
    top_value = drawn % level_count
    reach_top = (slots == 2) & (columns == BOXDEV - 1)
    top_value = jnp.where(reach_top, level_count - 1, top_value)
    value = jnp.where(level_every == LOCAL, top_value, close_value)
    burden = jax.random.randint(key_load, (devices,), 2, 8)
    ceiling = jnp.repeat(burden, BOXDEV)[None, :]
    kept = jax.random.randint(key_keep, (NFAR, FARCOLS), 0, 8) < ceiling
    kept = (kept | reach_close | reach_top) & jnp.logical_not((slots == 0) & (columns == 0))
    return jnp.where(kept, value, -1).astype(jnp.int32)


def steps_of(own_key, dims, cuts, smallest, high):
    level = 1.0
    for axis_at, parts in cuts:
        steps = jax.random.uniform(jax.random.fold_in(jax.random.fold_in(own_key, 6), axis_at), (parts,), jnp.float32, smallest / len(cuts), high / len(cuts))
        level = level * jnp.repeat(jnp.exp(steps), dims[axis_at] // parts).reshape((-1,) + (1,) * (len(dims) - 1 - axis_at))
    return level


def gaussian(stream_key, extent, deviation, most, cuts=(), kind=jnp.bfloat16):
    factor_of = steps_of(stream_key, extent, cuts, -0.22, 0.18) if cuts else 1.0
    values = jax.random.normal(stream_key, extent, jnp.float32) * deviation * factor_of
    return jnp.minimum(jnp.maximum(values, -most), most).astype(kind)


def setup_inputs(seed: int = 0) -> dict:
    key_of = jax.random.split(jax.random.key(seed), 12)
    field = gaussian(key_of[0], (CELLS, NBOX), 1.0, 6.0, ((1, 256),), jnp.float32)
    contrast = jnp.clip(jnp.exp(math.log(2.0) - 2.9957323 * jax.random.uniform(key_of[1], (CELLS, NBOX), jnp.float32) ** steps_of(key_of[1], (CELLS, NBOX), ((1, 256),), -0.2, 0.2)), 0.1, 2.0)
    incident = gaussian(key_of[2], (CELLS, NBOX), 1.0, 6.0, ((1, 256),), jnp.float32)
    near_lists = draw_near_lists(jax.random.fold_in(key_of[11], 71), 0)
    far_lists = draw_far_lists(jax.random.fold_in(key_of[11], 71), 0)
    near_mats = gaussian(key_of[5], (NNEAR, CELLS, CELLS), (CELLS * NNEAR) ** -0.5, 0.15625, (), jnp.float32)
    far_mats = gaussian(key_of[6], (NFAR, TERMS, TERMS), (TERMS * NFAR // 2) ** -0.5, 0.0625, (), jnp.float32)
    up_mats = gaussian(key_of[7], (8, TERMS, TERMS), (8 * TERMS) ** -0.5, 0.3125, (), jnp.float32)
    down_mats = gaussian(key_of[8], (8, TERMS, TERMS), TERMS ** -0.5, 0.875, (), jnp.float32)
    moment_map = gaussian(key_of[9], (TERMS, CELLS), CELLS ** -0.5, 0.75, (), jnp.float32)
    local_map = gaussian(key_of[10], (CELLS, TERMS), (TERMS * (LOCAL + 1)) ** -0.5, 0.5, (), jnp.float32)
    return {"field": field, "contrast": contrast, "incident": incident, "near_lists": near_lists, "far_lists": far_lists, "near_mats": near_mats, "far_mats": far_mats, "up_mats": up_mats, "down_mats": down_mats, "moment_map": moment_map, "local_map": local_map}


HIGHEST_PRECISION = lax.Precision.HIGHEST


def upward(moments, up_mats):
    children = moments.reshape(moments.shape[0], -1, 8)
    return jnp.einsum("cst,tjc->sj", up_mats, children, precision=HIGHEST_PRECISION)


def downward(parents, down_mats):
    children = jnp.einsum("cst,tj->sjc", down_mats, parents, precision=HIGHEST_PRECISION)
    return children.reshape(parents.shape[0], -1)


def slot_sum(values, lists, mats):
    def add_slot(total, inputs):
        slot_row, matrix = inputs
        valid = slot_row >= 0
        picked = jnp.where(valid[None, :], values[:, jnp.where(valid, slot_row, 0)], 0.0)
        return total + jnp.dot(matrix, picked, precision=HIGHEST_PRECISION), None

    start_total = jnp.zeros((mats.shape[1], lists.shape[1]), jnp.float32)
    total, _ = lax.scan(add_slot, start_total, (lists, mats))
    return total


def reference(field, contrast, incident, near_lists, far_lists, near_mats, far_mats, up_mats, down_mats, moment_map, local_map):
    devices = N_GROUP * N_OWNER
    source = contrast * field
    leaf_ids = jnp.arange(NBOX, dtype=jnp.int32)[None, :]
    near_boxes = jnp.where(near_lists >= 0, leaf_ids + near_lists - NEARW, -1).astype(jnp.int32)
    near_field = slot_sum(source, near_boxes, near_mats)
    moments = [jnp.dot(moment_map, source, precision=HIGHEST_PRECISION)]
    for level in range(LOCAL):
        moments.append(upward(moments[-1], up_mats))
    spans = [TOPS * 8 ** (LOCAL - level) for level in range(LOCAL + 1)]
    offsets = [sum(spans[:level]) for level in range(LOCAL + 1)]
    table = far_lists.reshape(NFAR, devices, BOXDEV)
    expansion = None
    for level in range(LOCAL, -1, -1):
        level_lists = table[:, :, offsets[level]:offsets[level] + spans[level]].reshape(NFAR, spans[level] * devices)
        if level < LOCAL:
            own_ids = jnp.arange(spans[level] * devices, dtype=jnp.int32)[None, :]
            level_lists = jnp.where(level_lists >= 0, own_ids + level_lists - spans[level] // 2, -1).astype(jnp.int32)
        far_term = slot_sum(moments[level], level_lists, far_mats)
        if level == LOCAL:
            expansion = far_term
        else:
            expansion = far_term + downward(expansion, down_mats)
    far_field = jnp.dot(local_map, expansion, precision=HIGHEST_PRECISION)
    return incident + near_field + far_field
```

```python
import functools

import jax
import jax.numpy as jnp
from jax import lax
from jax.experimental import pallas as pl
from jax.experimental.pallas import tpu as pltpu
from jax.sharding import PartitionSpec as P

f32, bf16, i32 = jnp.float32, jnp.bfloat16, jnp.int32
MESH = pl.DeviceIdType.MESH
HIGHEST = lax.Precision.HIGHEST

LEAVES = 128
TERMS = 49
SLOTS = 316
WIDE = 384
GROUP = 7
NGROUP = TERMS // GROUP
ROWS = 144
BLOCK = 8


def split(x):
    hi = x.astype(bf16)
    return hi, (x - hi.astype(f32)).astype(bf16)


def take(source, index):
    return jnp.take_along_axis(source, index, axis=1, mode="promise_in_bounds")


def nt(a, b):
    return lax.dot_general(a, b, (((1,), (1,)), ((), ())), precision=HIGHEST, preferred_element_type=f32)


def rows_of_children(ref, count):
    return jnp.concatenate([ref[pl.ds(c, count, stride=8), :] for c in range(8)], axis=1)


def pad_mats(x):
    r, c = x.shape
    x = jnp.concatenate([x, jnp.zeros((r, WIDE - c), x.dtype)], 1)
    return jnp.concatenate([x, jnp.zeros((64 - r, WIDE), x.dtype)], 0)


def prepare_lists(lists, index, code, index2, code2):
    index[:, 256:WIDE] = jnp.zeros((ROWS, 128), i32)
    code[:, 256:WIDE] = jnp.full((ROWS, 128), 2, i32)
    index2[:, :, 256:WIDE] = jnp.zeros((2, 8, 128), i32)
    code2[:, :, 256:WIDE] = jnp.full((2, 8, 128), 4, i32)
    for lo, hi in ((0, 128), (128, 256), (256, SLOTS)):
        e = lists[0:ROWS, lo:hi]
        row = lax.broadcasted_iota(i32, e.shape, 0)
        i = jnp.where(row < LEAVES, row, row - LEAVES) + e
        valid = e >= 0
        index[:, lo:hi] = jnp.where(valid, i & 127, 0)
        code[:, lo:hi] = jnp.where(valid, jnp.where((e == LEAVES), 1, 0), 2)
        for j in range(2):
            e = jnp.broadcast_to(lists[ROWS + j : ROWS + j + 1, lo:hi], (8, hi - lo))
            index2[j, :, lo:hi] = jnp.where(e >= 0, (e >> 1) & 127, 0)
            code2[j, :, lo:hi] = jnp.where(e >= 0, (e & 1) * 2 + (e >> 8), 4)


def prepare_mats(mats, weights, g):
    for ti in range(GROUP):
        x = mats[g * GROUP + ti]
        hi = x.astype(bf16).astype(f32)
        cols = slice(ti * WIDE, (ti + 1) * WIDE)
        weights[g, 0:64, cols] = pad_mats(x).astype(bf16)
        weights[g, 64:128, cols] = pad_mats(x - hi).astype(bf16)


def pick_group(e0b, e1b, xs, index, code, picked, g):
    lane = lax.broadcasted_iota(i32, (16, 128), 1)
    sub = lax.broadcasted_iota(i32, (16, 128), 0)
    for bt in range(9):
        rows = slice(bt * 16, bt * 16 + 16)
        sources = []
        for ti in range(GROUP):
            t = g * GROUP + ti
            if bt < 8:
                own = e0b[t, :, 0:128]
                far = e0b[t, :, 128:256]
                both = [jnp.where(lane[0:8] >= sub[0:8] + (bt * 16 + h * 8), own, far) for h in range(2)]
            else:
                both = [e1b[t], e1b[t]]
            sources.append(jnp.concatenate(both, 0))
        for kt in range(3):
            i = index[rows, kt * 128 : kt * 128 + 128]
            k = code[rows, kt * 128 : kt * 128 + 128]
            for ti in range(GROUP):
                x = take(sources[ti], i)
                if bt < 8:
                    last = xs[rows, ti * 128 : ti * 128 + 128]
                    x = jnp.where(k == 0, x, jnp.where(k == 1, last, 0.0))
                else:
                    x = jnp.where(k == 0, x, 0.0)
                hi, lo = split(x)
                cols = slice(ti * WIDE + kt * 128, ti * WIDE + kt * 128 + 128)
                picked[bt * 16 : bt * 16 + 16, cols] = hi
                picked[ROWS + bt * 16 : ROWS + bt * 16 + 16, cols] = lo


def spread_group(ends, xs, g):
    row = lax.broadcasted_iota(i32, (256, GROUP * 128), 0) & 127
    col = lax.broadcasted_iota(i32, (256, GROUP * 128), 1) >> 7
    select = jnp.where(row == col + g * GROUP, 1.0, 0.0).astype(bf16)
    xs[...] = jnp.dot(ends, select, preferred_element_type=f32)


def dot_group(picked, weights, g):
    return lax.dot_general(picked[...], weights[g], (((1,), (1,)), ((), ())), preferred_element_type=f32)


def kernel(
    shape,
    field, contrast, incident, near_lists, lists, near_mats, far_mats, up, down, moment_map, local_t,
    out,
    mats, weights, picked_a, picked_b, xs_a, xs_b, index, code, index2, code2, total,
    rolled, from_left, from_right, up_cat, down_cat, m0_own, m0_ext, m1_own, m2_own, mine, tops,
    e0, e0b, e1b, near_all, p2, x2, x1,
    mat_sem, halo_send, halo_recv, send1, recv1, send2, recv2, own_sem,
):
    n_group, n_owner = shape
    n = n_group * n_owner
    blocks = n // BLOCK
    rank = lax.axis_index("group") * n_owner + lax.axis_index("owner")

    def at(r):
        return (r // n_owner, r % n_owner)

    left, right = (rank + n - 1) % n, (rank + 1) % n
    base = rank // BLOCK * BLOCK
    slot = rank % BLOCK

    if n < 256:
        tops[...] = jnp.zeros_like(tops)

    def start_mats(t, _):
        pltpu.make_async_copy(far_mats.at[:, t, :], mats.at[t], mat_sem.at[t]).start()
        return 0

    lax.fori_loop(0, TERMS, start_mats, 0)

    def peer1(d):
        return base + (slot + d) % BLOCK

    def peer2(d):
        return (rank + d * BLOCK) % n

    barrier = pltpu.get_barrier_semaphore()
    pl.semaphore_signal(barrier, inc=1, device_id=at(left), device_id_type=MESH)
    pl.semaphore_signal(barrier, inc=1, device_id=at(right), device_id_type=MESH)

    def greet1(d, _):
        pl.semaphore_signal(barrier, inc=1, device_id=at(peer1(d)), device_id_type=MESH)
        return 0

    def greet2(d, _):
        pl.semaphore_signal(barrier, inc=1, device_id=at(peer2(d)), device_id_type=MESH)
        return 0

    lax.fori_loop(1, BLOCK, greet1, 0)
    lax.fori_loop(1, blocks, greet2, 0)

    source = contrast[...] * field[...]
    own_rolled = pltpu.roll(source, 64, 1)
    rolled[...] = own_rolled
    up_cat[...] = jnp.zeros_like(up_cat)
    down_cat[...] = jnp.zeros_like(down_cat)
    for c in range(8):
        up_cat[:, c * 128 : c * 128 + TERMS] = up[:, c, :]
        down_cat[:, c * 128 : c * 128 + TERMS] = down[:, c, :]
    m0_own[...] = jnp.zeros_like(m0_own)
    m1_own[...] = jnp.zeros_like(m1_own)
    m2_own[...] = jnp.zeros_like(m2_own)
    x2[...] = jnp.zeros_like(x2)
    x1[...] = jnp.zeros_like(x1)
    e1b[...] = jnp.zeros_like(e1b)
    m0_ext[...] = jnp.zeros_like(m0_ext)
    m0_own[:, 0:TERMS] = nt(source.T, moment_map[...])
    m1_own[:, 0:TERMS] = nt(rows_of_children(m0_own, 16), up_cat[...])
    m2_own[0:2, 0:TERMS] = nt(rows_of_children(m1_own, 2), up_cat[...])
    mine[...] = m2_own[0:1, :] + pltpu.roll(m2_own[1:2, :], 64, 1)

    pl.semaphore_wait(barrier, 2 + (BLOCK - 1) + (blocks - 1))
    own_copy = pltpu.make_async_copy(mine, tops.at[pl.ds(rank, 1), :], own_sem)
    own_copy.start()

    def first(d, sender):
        return pltpu.make_async_remote_copy(
            src_ref=mine, dst_ref=tops.at[pl.ds(sender, 1), :],
            send_sem=send1.at[d], recv_sem=recv1.at[d], device_id=at(peer1(d)), device_id_type=MESH)

    def second(d, owner):
        block = pl.ds(owner // BLOCK * BLOCK, BLOCK)
        return pltpu.make_async_remote_copy(
            src_ref=tops.at[block, :], dst_ref=tops.at[block, :],
            send_sem=send2.at[d], recv_sem=recv2.at[d], device_id=at(peer2(d)), device_id_type=MESH)

    lax.fori_loop(1, BLOCK, lambda d, _: (first(d, rank).start(), 0)[1], 0)
    to_right = pltpu.make_async_remote_copy(
        src_ref=rolled, dst_ref=from_left, send_sem=halo_send.at[0], recv_sem=halo_recv.at[0],
        device_id=at(right), device_id_type=MESH)
    to_left = pltpu.make_async_remote_copy(
        src_ref=rolled, dst_ref=from_right, send_sem=halo_send.at[1], recv_sem=halo_recv.at[1],
        device_id=at(left), device_id_type=MESH)
    to_right.start()
    to_left.start()

    prepare_lists(lists, index, code, index2, code2)
    own_copy.wait()
    lax.fori_loop(
        1, BLOCK, lambda d, _: (first(d, base + (slot + BLOCK - d) % BLOCK).wait_recv(), 0)[1], 0)
    lax.fori_loop(1, blocks, lambda d, _: (second(d, rank).start(), 0)[1], 0)

    def wait_mats(t, _):
        pltpu.make_async_copy(far_mats.at[:, t, :], mats.at[t], mat_sem.at[t]).wait()
        return 0

    lax.fori_loop(0, TERMS, wait_mats, 0)
    lax.fori_loop(0, NGROUP, lambda g, _: (prepare_mats(mats, weights, g), 0)[1], 0)

    to_right.wait()
    to_left.wait()
    lane = lax.broadcasted_iota(i32, (64, 128), 1)
    ext_a = jnp.where(lane < 64, from_left[...], own_rolled)
    ext_b = jnp.where(lane < 64, own_rolled, from_right[...])
    ext = jnp.concatenate([ext_a, ext_b], 1)
    e0[...] = jnp.dot(moment_map[...], ext, precision=HIGHEST, preferred_element_type=f32)
    for t in range(TERMS):
        e0b[t] = jnp.broadcast_to(e0[t : t + 1, :], (8, 256))
    m0_ext[0:128, 0:TERMS] = e0[:, 0:128].T
    m0_ext[128:256, 0:TERMS] = e0[:, 128:256].T
    e1 = nt(up_cat[...], rows_of_children(m0_ext, 32))
    for t in range(TERMS):
        e1b[t, :, 0:32] = jnp.broadcast_to(e1[t : t + 1, :], (8, 32))
    ends = jnp.concatenate(split(m0_ext[128:256, :]), 1)

    s_hi, s_lo = split(ext)
    n_hi, n_lo = split(near_mats[...].reshape(27 * 64, 64))
    near_all[...] = jnp.dot(
        jnp.concatenate([n_hi, n_hi, n_lo], 1), jnp.concatenate([s_hi, s_lo, s_hi], 0), preferred_element_type=f32)
    near = incident[...]
    for k in range(27):
        e = jnp.broadcast_to(near_lists[k : k + 1, :], (64, 128))
        i = e + lane
        valid = e >= 0
        m = jnp.where(valid, i & 127, 0)
        rows = slice(k * 64, k * 64 + 64)
        near = near + jnp.where(
            valid, jnp.where(i < 128, take(near_all[rows, 0:128], m), take(near_all[rows, 128:256], m)), 0.0)
    out[...] = near

    total[...] = jnp.zeros_like(total)
    spread_group(ends, xs_a, 0)
    pick_group(e0b, e1b, xs_a, index, code, picked_a, 0)

    def far_pair(h, _):
        spread_group(ends, xs_b, 2 * h + 1)
        part = dot_group(picked_a, weights, 2 * h)
        pick_group(e0b, e1b, xs_b, index, code, picked_b, 2 * h + 1)
        total[...] += part
        spread_group(ends, xs_a, 2 * h + 2)
        part = dot_group(picked_b, weights, 2 * h + 1)
        pick_group(e0b, e1b, xs_a, index, code, picked_a, 2 * h + 2)
        total[...] += part
        return 0

    lax.fori_loop(0, NGROUP // 2, far_pair, 0)
    total[...] += dot_group(picked_a, weights, NGROUP - 1)
    both = total[0:ROWS, :] + total[ROWS : 2 * ROWS, :]
    terms = both + pltpu.roll(both, 64, 1)

    lax.fori_loop(1, blocks, lambda d, _: (second(d, (rank + n - d * BLOCK) % n).wait_recv(), 0)[1], 0)
    lax.fori_loop(1, BLOCK, lambda d, _: (first(d, rank).wait_send(), 0)[1], 0)
    lax.fori_loop(1, blocks, lambda d, _: (second(d, rank).wait_send(), 0)[1], 0)
    every = tops[...].T
    for j in range(2):
        for kt in range(3):
            cols = slice(kt * 128, kt * 128 + 128)
            i = jnp.concatenate([index2[j, :, cols]] * 7, 0)
            k = jnp.concatenate([code2[j, :, cols]] * 7, 0)
            x = jnp.zeros((56, 128), f32)
            for q in range(4):
                part = every[(q >> 1) * 64 : (q >> 1) * 64 + 56, (q & 1) * 128 : (q & 1) * 128 + 128]
                x = jnp.where(k == q, take(part, i), x)
            p2[j, :, cols] = x

    sums = [jnp.zeros((TERMS, 128), f32)] * 2 + [jnp.zeros((TERMS, SLOTS - 256), f32)] * 2
    for t in range(TERMS):
        a, b, c = mats[t, :, 0:128], mats[t, :, 128:256], mats[t, :, 256:SLOTS]
        for j in range(2):
            sums[j] = sums[j] + (a * p2[j, t : t + 1, 0:128] + b * p2[j, t : t + 1, 128:256])
            sums[2 + j] = sums[2 + j] + c * p2[j, t : t + 1, 256:SLOTS]
    for j in range(2):
        x2[j * 8 : j * 8 + 8, 0:TERMS] = nt(jnp.ones((8, 128), f32), sums[j]) + nt(
            jnp.ones((8, SLOTS - 256), f32), sums[2 + j])

    def children(parents, count):
        sub = lax.broadcasted_iota(i32, (count, 128), 0) & 7
        spread = jnp.concatenate([jnp.where(sub == c, parents, 0.0) for c in range(8)], 1)
        return nt(spread, down_cat[...])

    x1[:, 0:TERMS] = terms[LEAVES:ROWS, 0:TERMS] + children(x2[...], 16)
    parents = jnp.concatenate([jnp.broadcast_to(x1[j : j + 1, :], (8, 128)) for j in range(16)], 0)
    x0 = terms[0:LEAVES, 0:TERMS] + children(parents, 128)
    out[...] += nt(local_t[...].T, x0)


def body(mesh_shape, field, contrast, incident, near_lists, far_lists, near_mats, far_mats, up_mats, down_mats,
         moment_map, local_map):
    vmem = pl.BlockSpec(memory_space=pltpu.VMEM)
    n = mesh_shape[0] * mesh_shape[1]
    dma = pltpu.SemaphoreType.DMA
    call = pl.pallas_call(
        functools.partial(kernel, mesh_shape),
        out_shape=jax.ShapeDtypeStruct((64, LEAVES), f32),
        in_specs=[vmem] * 6 + [pl.BlockSpec(memory_space=pl.ANY)] + [vmem] * 4,
        out_specs=vmem,
        scratch_shapes=[
            pltpu.VMEM((TERMS, TERMS, SLOTS), f32),
            pltpu.VMEM((NGROUP, 128, GROUP * WIDE), bf16),
            pltpu.VMEM((2 * ROWS, GROUP * WIDE), bf16),
            pltpu.VMEM((2 * ROWS, GROUP * WIDE), bf16),
            pltpu.VMEM((LEAVES, GROUP * 128), f32),
            pltpu.VMEM((LEAVES, GROUP * 128), f32),
            pltpu.VMEM((ROWS, WIDE), i32),
            pltpu.VMEM((ROWS, WIDE), i32),
            pltpu.VMEM((2, 8, WIDE), i32),
            pltpu.VMEM((2, 8, WIDE), i32),
            pltpu.VMEM((2 * ROWS, 128), f32),
            pltpu.VMEM((64, 128), f32),
            pltpu.VMEM((64, 128), f32),
            pltpu.VMEM((64, 128), f32),
            pltpu.VMEM((TERMS, 1024), f32),
            pltpu.VMEM((TERMS, 1024), f32),
            pltpu.VMEM((128, 128), f32),
            pltpu.VMEM((256, 128), f32),
            pltpu.VMEM((16, 128), f32),
            pltpu.VMEM((8, 128), f32),
            pltpu.VMEM((1, 128), f32),
            pltpu.VMEM((256, 128), f32),
            pltpu.VMEM((TERMS, 256), f32),
            pltpu.VMEM((TERMS, 8, 256), f32),
            pltpu.VMEM((TERMS, 8, 128), f32),
            pltpu.VMEM((27 * 64, 256), f32),
            pltpu.VMEM((2, 56, WIDE), f32),
            pltpu.VMEM((16, 128), f32),
            pltpu.VMEM((16, 128), f32),
            dma((TERMS,)), dma((2,)), dma((2,)), dma((BLOCK,)), dma((BLOCK,)),
            dma((n // BLOCK + 1,)), dma((n // BLOCK + 1,)), dma,
        ],
        compiler_params=pltpu.CompilerParams(
            collective_id=0, has_side_effects=True, vmem_limit_bytes=48 * 2**20),
    )
    return call(
        field, contrast, incident, near_lists, far_lists.T, near_mats, jnp.transpose(far_mats, (1, 2, 0)),
        jnp.transpose(up_mats, (1, 0, 2)), jnp.transpose(down_mats, (1, 0, 2)), moment_map, local_map.T)


def solution(mesh):
    line = P(None, ("group", "owner"))
    return jax.shard_map(
        functools.partial(body, (mesh.shape["group"], mesh.shape["owner"])), mesh=mesh,
        in_specs=(line,) * 5 + (P(),) * 6, out_specs=line, check_vma=False)
```

```python
import functools

import jax
import jax.numpy as jnp
from jax import lax
from jax.experimental import pallas as pl
from jax.experimental.pallas import tpu as pltpu
from jax.sharding import PartitionSpec as P

f32, bf16, i32 = jnp.float32, jnp.bfloat16, jnp.int32
MESH = pl.DeviceIdType.MESH
HIGHEST = lax.Precision.HIGHEST

LEAVES = 128
TERMS = 49
SLOTS = 316
WIDE = 384
GROUP = 7
NGROUP = TERMS // GROUP
ROWS = 144
BLOCK = 8


def split(x):
    hi = x.astype(bf16)
    return hi, (x - hi.astype(f32)).astype(bf16)


def take(source, index):
    return jnp.take_along_axis(source, index, axis=1, mode="promise_in_bounds")


def nt(a, b):
    return lax.dot_general(a, b, (((1,), (1,)), ((), ())), precision=HIGHEST, preferred_element_type=f32)


def nt3(a, b_parts):
    rows = a.shape[0]
    both = lax.dot_general(
        jnp.concatenate(split(a), 0), b_parts, (((1,), (1,)), ((), ())), preferred_element_type=f32)
    both = both[0:rows] + both[rows : 2 * rows]
    return both + pltpu.roll(both, 64, 1)


def rows_of_children(ref, count):
    return jnp.concatenate([ref[pl.ds(c, count, stride=8), :] for c in range(8)], axis=1)


def pad_mats(x):
    r, c = x.shape
    x = jnp.concatenate([x, jnp.zeros((r, WIDE - c), x.dtype)], 1)
    return jnp.concatenate([x, jnp.zeros((64 - r, WIDE), x.dtype)], 0)


def prepare_lists(lists, index, code, index2, code2, blocks):
    index[:, 256:WIDE] = jnp.zeros((ROWS, 128), i32)
    code[:, 256:WIDE] = jnp.full((ROWS, 128), 2, i32)
    index2[:, :, 256:WIDE] = jnp.zeros((2, 8, 128), i32)
    code2[:, :, 256:WIDE] = jnp.full((2, 8, 128), 4, i32)
    for lo, hi in ((0, 128), (128, 256), (256, SLOTS)):
        e = lists[0:ROWS, lo:hi]
        row = lax.broadcasted_iota(i32, e.shape, 0)
        i = jnp.where(row < LEAVES, row, row - LEAVES) + e
        valid = e >= 0
        index[:, lo:hi] = jnp.where(valid, i & 127, 0)
        code[:, lo:hi] = jnp.where(valid, jnp.where((e == LEAVES), 1, 0), 2)
        for j in range(2):
            e = jnp.broadcast_to(lists[ROWS + j : ROWS + j + 1, lo:hi], (8, hi - lo))
            place = ((e >> 1) & (BLOCK - 1)) * blocks + (e >> 4)
            index2[j, :, lo:hi] = jnp.where(e >= 0, place & 127, 0)
            code2[j, :, lo:hi] = jnp.where(e >= 0, (e & 1) * 2 + (place >> 7), 4)


def prepare_mats(mats, weights, g):
    for ti in range(GROUP):
        x = mats[g * GROUP + ti]
        hi = x.astype(bf16).astype(f32)
        cols = slice(ti * WIDE, (ti + 1) * WIDE)
        weights[g, 0:64, cols] = pad_mats(x).astype(bf16)
        weights[g, 64:128, cols] = pad_mats(x - hi).astype(bf16)


def pick_group(e0b, e1b, xs, index, code, picked, g):
    lane = lax.broadcasted_iota(i32, (16, 128), 1)
    sub = lax.broadcasted_iota(i32, (16, 128), 0)
    for bt in range(9):
        rows = slice(bt * 16, bt * 16 + 16)
        sources = []
        for ti in range(GROUP):
            t = g * GROUP + ti
            if bt < 8:
                own = e0b[t, :, 0:128]
                far = e0b[t, :, 128:256]
                both = [jnp.where(lane[0:8] >= sub[0:8] + (bt * 16 + h * 8), own, far) for h in range(2)]
            else:
                both = [e1b[t], e1b[t]]
            sources.append(jnp.concatenate(both, 0))
        for kt in range(3):
            i = index[rows, kt * 128 : kt * 128 + 128]
            k = code[rows, kt * 128 : kt * 128 + 128]
            for ti in range(GROUP):
                x = take(sources[ti], i)
                if bt < 8:
                    last = xs[rows, ti * 128 : ti * 128 + 128]
                    x = jnp.where(k == 0, x, jnp.where(k == 1, last, 0.0))
                else:
                    x = jnp.where(k == 0, x, 0.0)
                hi, lo = split(x)
                cols = slice(ti * WIDE + kt * 128, ti * WIDE + kt * 128 + 128)
                picked[bt * 16 : bt * 16 + 16, cols] = hi
                picked[ROWS + bt * 16 : ROWS + bt * 16 + 16, cols] = lo


def spread_group(ends, xs, g):
    row = lax.broadcasted_iota(i32, (256, GROUP * 128), 0) & 127
    col = lax.broadcasted_iota(i32, (256, GROUP * 128), 1) >> 7
    select = jnp.where(row == col + g * GROUP, 1.0, 0.0).astype(bf16)
    xs[...] = jnp.dot(ends, select, preferred_element_type=f32)


def dot_group(picked, weights, g):
    return lax.dot_general(picked[...], weights[g], (((1,), (1,)), ((), ())), preferred_element_type=f32)


def kernel(
    shape,
    field_in, contrast_in, incident_in, near_lists_in, lists_in, near_mats_in, far_mats, up_in, down_in, map_in, local_in,
    out,
    field, contrast, incident, near_lists, lists, near_mats, up, down, moment_map, local_t,
    mats, weights, picked_a, picked_b, xs_a, xs_b, index, code, index2, code2, total,
    rolled, halves, up_cat, down_cat, down_parts, m0_own, m0_ext, m1_own, m2_own, mine, tops,
    e0, e0b, e1b, near_all, p2, x2, x1,
    in_sem, mat_sem, send, recv, send1, recv1, send2, recv2, own_sem,
):
    n_owner = shape[1]
    n = shape[0] * n_owner
    blocks = n // BLOCK
    rank = lax.axis_index("group") * n_owner + lax.axis_index("owner")
    slot, block = rank % BLOCK, rank // BLOCK
    has_left, has_right = rank > 0, rank < n - 1

    def at(r):
        return (r // n_owner, r % n_owner)

    def near_peer(d):
        return block * BLOCK + (slot + d) % BLOCK

    def line_peer(d):
        return (rank + d * BLOCK) % n

    pairs = (
        (field_in, field), (contrast_in, contrast), (map_in, moment_map), (up_in, up), (lists_in, lists),
        (near_mats_in, near_mats), (near_lists_in, near_lists), (incident_in, incident), (down_in, down),
        (local_in, local_t))
    loads = [pltpu.make_async_copy(a, b, in_sem.at[i]) for i, (a, b) in enumerate(pairs)]
    for load in loads[:4]:
        load.start()
    if n < 256:
        tops[...] = jnp.zeros_like(tops)

    @pl.when(rank == 0)
    def _():
        halves[0] = jnp.zeros((64, LEAVES), f32)

    @pl.when(rank == n - 1)
    def _():
        halves[1] = jnp.zeros((64, LEAVES), f32)

    barrier = pltpu.get_barrier_semaphore()

    @pl.when(has_left)
    def _():
        pl.semaphore_signal(barrier, inc=1, device_id=at(rank - 1), device_id_type=MESH)

    @pl.when(has_right)
    def _():
        pl.semaphore_signal(barrier, inc=1, device_id=at(rank + 1), device_id_type=MESH)

    def greet_line(d, _):
        pl.semaphore_signal(barrier, inc=1, device_id=at(line_peer(d)), device_id_type=MESH)
        return 0

    def greet_near(d, _):
        pl.semaphore_signal(barrier, inc=1, device_id=at(near_peer(d)), device_id_type=MESH)
        return 0

    lax.fori_loop(1, blocks, greet_line, 0)
    lax.fori_loop(1, BLOCK, greet_near, 0)

    def start_mats(t, _):
        pltpu.make_async_copy(far_mats.at[:, t, :], mats.at[t], mat_sem.at[t]).start()
        return 0

    def wait_mats(t, _):
        pltpu.make_async_copy(far_mats.at[:, t, :], mats.at[t], mat_sem.at[t]).wait()
        return 0

    for load in loads[4:]:
        load.start()
    lax.fori_loop(0, TERMS, start_mats, 0)
    for ref in (up_cat, down_cat, m0_own, m0_ext, m1_own, m2_own, x2, x1, e1b, total):
        ref[...] = jnp.zeros_like(ref)

    for load in loads[:4]:
        load.wait()
    source = contrast[...] * field[...]
    rolled[...] = pltpu.roll(source, 64, 1)
    for c in range(8):
        up_cat[:, c * 128 : c * 128 + TERMS] = up[:, c, :]
    m0_own[:, 0:TERMS] = nt(source.T, moment_map[...])
    m1_own[:, 0:TERMS] = nt(rows_of_children(m0_own, 16), up_cat[...])
    m2_own[0:2, 0:TERMS] = nt(rows_of_children(m1_own, 2), up_cat[...])
    mine[...] = m2_own[0:1, :] + pltpu.roll(m2_own[1:2, :], 64, 1)
    own_copy = pltpu.make_async_copy(mine, tops.at[pl.ds(slot * blocks + block, 1), :], own_sem)
    own_copy.start()

    def halo(side, target):
        return pltpu.make_async_remote_copy(
            src_ref=rolled, dst_ref=halves.at[side], send_sem=send.at[side], recv_sem=recv.at[side],
            device_id=at(target), device_id_type=MESH)

    def first(d, sender):
        return pltpu.make_async_remote_copy(
            src_ref=mine, dst_ref=tops.at[pl.ds(slot * blocks + sender // BLOCK, 1), :],
            send_sem=send1.at[d], recv_sem=recv1.at[d], device_id=at(line_peer(d)), device_id_type=MESH)

    def second(d, owner):
        part = tops.at[pl.ds(owner % BLOCK * blocks, blocks), :]
        return pltpu.make_async_remote_copy(
            src_ref=part, dst_ref=part,
            send_sem=send2.at[d], recv_sem=recv2.at[d], device_id=at(near_peer(d)), device_id_type=MESH)

    def send_all():
        others = (BLOCK - 1) + (blocks - 1)
        inside = jnp.logical_and(has_left, has_right)

        @pl.when(inside)
        def _():
            pl.semaphore_wait(barrier, others + 2)

        @pl.when(jnp.logical_not(inside))
        def _():
            pl.semaphore_wait(barrier, others + 1)

        @pl.when(has_right)
        def _():
            halo(0, rank + 1).start()

        @pl.when(has_left)
        def _():
            halo(1, rank - 1).start()

        lax.fori_loop(1, blocks, lambda d, _: (first(d, rank).start(), 0)[1], 0)

    @pl.when(rank >= n // 2)
    def _():
        send_all()

    for load in loads[4:]:
        load.wait()
    for c in range(8):
        down_cat[:, c * 128 : c * 128 + TERMS] = down[:, c, :]
    d_hi = down_cat[...].astype(bf16).astype(f32)
    rest = jnp.zeros((64 - TERMS, 1024), f32)
    down_parts[...] = jnp.concatenate([d_hi, rest, down_cat[...] - d_hi, rest], 0).astype(bf16)
    prepare_lists(lists, index, code, index2, code2, blocks)
    lax.fori_loop(0, TERMS, wait_mats, 0)
    lax.fori_loop(0, NGROUP, lambda g, _: (prepare_mats(mats, weights, g), 0)[1], 0)

    @pl.when(rank < n // 2)
    def _():
        send_all()

    @pl.when(has_right)
    def _():
        halo(0, rank + 1).wait_send()

    @pl.when(has_left)
    def _():
        halo(1, rank - 1).wait_send()

    @pl.when(has_left)
    def _():
        halo(0, rank).wait_recv()

    @pl.when(has_right)
    def _():
        halo(1, rank).wait_recv()

    lane = lax.broadcasted_iota(i32, (64, 128), 1)
    ext = jnp.concatenate(
        [jnp.where(lane < 64, halves[0], rolled[...]), jnp.where(lane < 64, rolled[...], halves[1])], 1)
    e0[...] = jnp.dot(moment_map[...], ext, precision=HIGHEST, preferred_element_type=f32)
    for t in range(TERMS):
        e0b[t] = jnp.broadcast_to(e0[t : t + 1, :], (8, 256))
    m0_ext[0:128, 0:TERMS] = e0[:, 0:128].T
    m0_ext[128:256, 0:TERMS] = e0[:, 128:256].T
    e1 = nt(up_cat[...], rows_of_children(m0_ext, 32))
    for t in range(TERMS):
        e1b[t, :, 0:32] = jnp.broadcast_to(e1[t : t + 1, :], (8, 32))
    ends = jnp.concatenate(split(m0_ext[128:256, :]), 1)

    s_hi, s_lo = split(ext)
    n_hi, n_lo = split(near_mats[...].reshape(27 * 64, 64))
    near_all[...] = jnp.dot(
        jnp.concatenate([n_hi, n_hi, n_lo], 1), jnp.concatenate([s_hi, s_lo, s_hi], 0), preferred_element_type=f32)
    near = incident[...]
    for k in range(27):
        e = jnp.broadcast_to(near_lists[k : k + 1, :], (64, 128))
        i = e + lane
        valid = e >= 0
        m = jnp.where(valid, i & 127, 0)
        rows = slice(k * 64, k * 64 + 64)
        near = near + jnp.where(
            valid, jnp.where(i < 128, take(near_all[rows, 0:128], m), take(near_all[rows, 128:256], m)), 0.0)
    out[...] = near

    own_copy.wait()
    lax.fori_loop(1, blocks, lambda d, _: (first(d, (rank + n - d * BLOCK) % n).wait_recv(), 0)[1], 0)
    lax.fori_loop(1, BLOCK, lambda d, _: (second(d, rank).start(), 0)[1], 0)

    spread_group(ends, xs_a, 0)
    pick_group(e0b, e1b, xs_a, index, code, picked_a, 0)

    def far_pair(h, _):
        spread_group(ends, xs_b, 2 * h + 1)
        part = dot_group(picked_a, weights, 2 * h)
        pick_group(e0b, e1b, xs_b, index, code, picked_b, 2 * h + 1)
        total[...] += part
        spread_group(ends, xs_a, 2 * h + 2)
        part = dot_group(picked_b, weights, 2 * h + 1)
        pick_group(e0b, e1b, xs_a, index, code, picked_a, 2 * h + 2)
        total[...] += part
        return 0

    lax.fori_loop(0, NGROUP // 2, far_pair, 0)
    total[...] += dot_group(picked_a, weights, NGROUP - 1)
    both = total[0:ROWS, :] + total[ROWS : 2 * ROWS, :]
    terms = both + pltpu.roll(both, 64, 1)

    lax.fori_loop(1, blocks, lambda d, _: (first(d, rank).wait_send(), 0)[1], 0)
    lax.fori_loop(1, BLOCK, lambda d, _: (second(d, rank).wait_send(), 0)[1], 0)
    lax.fori_loop(
        1, BLOCK, lambda d, _: (second(d, block * BLOCK + (slot + BLOCK - d) % BLOCK).wait_recv(), 0)[1], 0)
    every = tops[...].T
    for j in range(2):
        for kt in range(3):
            cols = slice(kt * 128, kt * 128 + 128)
            i = jnp.concatenate([index2[j, :, cols]] * 7, 0)
            k = jnp.concatenate([code2[j, :, cols]] * 7, 0)
            x = jnp.zeros((56, 128), f32)
            for q in range(4):
                part = every[(q >> 1) * 64 : (q >> 1) * 64 + 56, (q & 1) * 128 : (q & 1) * 128 + 128]
                x = jnp.where(k == q, take(part, i), x)
            p2[j, :, cols] = x

    sums = [jnp.zeros((TERMS, 128), f32)] * 2 + [jnp.zeros((TERMS, SLOTS - 256), f32)] * 2
    for t in range(TERMS):
        a, b, c = mats[t, :, 0:128], mats[t, :, 128:256], mats[t, :, 256:SLOTS]
        for j in range(2):
            sums[j] = sums[j] + (a * p2[j, t : t + 1, 0:128] + b * p2[j, t : t + 1, 128:256])
            sums[2 + j] = sums[2 + j] + c * p2[j, t : t + 1, 256:SLOTS]
    for j in range(2):
        x2[j * 8 : j * 8 + 8, 0:TERMS] = nt(jnp.ones((8, 128), f32), sums[j]) + nt(
            jnp.ones((8, SLOTS - 256), f32), sums[2 + j])

    def children(parents, count):
        sub = lax.broadcasted_iota(i32, (count, 128), 0) & 7
        spread = jnp.concatenate([jnp.where(sub == c, parents, 0.0) for c in range(8)], 1)
        return nt3(spread, down_parts[...])[:, 0:TERMS]

    x1[:, 0:TERMS] = terms[LEAVES:ROWS, 0:TERMS] + children(x2[...], 16)
    parents = jnp.concatenate([jnp.broadcast_to(x1[j : j + 1, :], (8, 128)) for j in range(16)], 0)
    x0 = terms[0:LEAVES, 0:TERMS] + children(parents, 128)
    out[...] += nt(local_t[...].T, x0)


def body(mesh_shape, field, contrast, incident, near_lists, far_lists, near_mats, far_mats, up_mats, down_mats,
         moment_map, local_map):
    vmem = pl.BlockSpec(memory_space=pltpu.VMEM)
    n = mesh_shape[0] * mesh_shape[1]
    dma = pltpu.SemaphoreType.DMA
    call = pl.pallas_call(
        functools.partial(kernel, mesh_shape),
        out_shape=jax.ShapeDtypeStruct((64, LEAVES), f32),
        in_specs=[pl.BlockSpec(memory_space=pl.ANY)] * 11,
        out_specs=vmem,
        scratch_shapes=[
            pltpu.VMEM((64, LEAVES), f32),
            pltpu.VMEM((64, LEAVES), f32),
            pltpu.VMEM((64, LEAVES), f32),
            pltpu.VMEM((27, LEAVES), i32),
            pltpu.VMEM((ROWS + 2, SLOTS), i32),
            pltpu.VMEM((27, 64, 64), f32),
            pltpu.VMEM((TERMS, 8, TERMS), f32),
            pltpu.VMEM((TERMS, 8, TERMS), f32),
            pltpu.VMEM((TERMS, 64), f32),
            pltpu.VMEM((TERMS, 64), f32),
            pltpu.VMEM((TERMS, TERMS, SLOTS), f32),
            pltpu.VMEM((NGROUP, 128, GROUP * WIDE), bf16),
            pltpu.VMEM((2 * ROWS, GROUP * WIDE), bf16),
            pltpu.VMEM((2 * ROWS, GROUP * WIDE), bf16),
            pltpu.VMEM((LEAVES, GROUP * 128), f32),
            pltpu.VMEM((LEAVES, GROUP * 128), f32),
            pltpu.VMEM((ROWS, WIDE), i32),
            pltpu.VMEM((ROWS, WIDE), i32),
            pltpu.VMEM((2, 8, WIDE), i32),
            pltpu.VMEM((2, 8, WIDE), i32),
            pltpu.VMEM((2 * ROWS, 128), f32),
            pltpu.VMEM((64, 128), f32),
            pltpu.VMEM((2, 64, 128), f32),
            pltpu.VMEM((TERMS, 1024), f32),
            pltpu.VMEM((TERMS, 1024), f32),
            pltpu.VMEM((128, 1024), bf16),
            pltpu.VMEM((128, 128), f32),
            pltpu.VMEM((256, 128), f32),
            pltpu.VMEM((16, 128), f32),
            pltpu.VMEM((8, 128), f32),
            pltpu.VMEM((1, 128), f32),
            pltpu.VMEM((256, 128), f32),
            pltpu.VMEM((TERMS, 256), f32),
            pltpu.VMEM((TERMS, 8, 256), f32),
            pltpu.VMEM((TERMS, 8, 128), f32),
            pltpu.VMEM((27 * 64, 256), f32),
            pltpu.VMEM((2, 56, WIDE), f32),
            pltpu.VMEM((16, 128), f32),
            pltpu.VMEM((16, 128), f32),
            dma((10,)), dma((TERMS,)), dma((2,)), dma((2,)), dma((n // BLOCK + 1,)), dma((n // BLOCK + 1,)),
            dma((BLOCK,)), dma((BLOCK,)), dma,
        ],
        compiler_params=pltpu.CompilerParams(
            collective_id=0, has_side_effects=True, vmem_limit_bytes=63 * 2**20),
    )
    return call(
        field, contrast, incident, near_lists, far_lists.T, near_mats, jnp.transpose(far_mats, (1, 2, 0)),
        jnp.transpose(up_mats, (1, 0, 2)), jnp.transpose(down_mats, (1, 0, 2)), moment_map, local_map.T)


def solution(mesh):
    line = P(None, ("group", "owner"))
    return jax.shard_map(
        functools.partial(body, (mesh.shape["group"], mesh.shape["owner"])), mesh=mesh,
        in_specs=(line,) * 5 + (P(),) * 6, out_specs=line, check_vma=False)
```

```python
import functools

import jax
import jax.numpy as jnp
from jax import lax
from jax.experimental import pallas as pl
from jax.experimental.pallas import tpu as pltpu
from jax.sharding import PartitionSpec as P

f32, bf16, i32 = jnp.float32, jnp.bfloat16, jnp.int32
MESH = pl.DeviceIdType.MESH
HIGHEST = lax.Precision.HIGHEST

LEAVES = 128
TERMS = 49
SLOTS = 316
WIDE = 384
GROUP = 7
NGROUP = TERMS // GROUP
ROWS = 144
FIRST_PAIRS = 1
BLOCK = 8


def split(x):
    hi = x.astype(bf16)
    return hi, (x - hi.astype(f32)).astype(bf16)


def take(source, index):
    return jnp.take_along_axis(source, index, axis=1, mode="promise_in_bounds")


def nt(a, b):
    return lax.dot_general(a, b, (((1,), (1,)), ((), ())), precision=HIGHEST, preferred_element_type=f32)


def nt3(a, b_parts):
    rows = a.shape[0]
    both = lax.dot_general(
        jnp.concatenate(split(a), 0), b_parts, (((1,), (1,)), ((), ())), preferred_element_type=f32)
    both = both[0:rows] + both[rows : 2 * rows]
    return both + pltpu.roll(both, 64, 1)


def rows_of_children(ref, count):
    return jnp.concatenate([ref[pl.ds(c, count, stride=8), :] for c in range(8)], axis=1)


def pad_mats(x):
    r, c = x.shape
    x = jnp.concatenate([x, jnp.zeros((r, WIDE - c), x.dtype)], 1)
    return jnp.concatenate([x, jnp.zeros((64 - r, WIDE), x.dtype)], 0)


def prepare_lists(lists, index, code, index2, code2, blocks):
    index[:, 256:WIDE] = jnp.zeros((ROWS, 128), i32)
    code[:, 256:WIDE] = jnp.full((ROWS, 128), 2, i32)
    index2[:, :, 256:WIDE] = jnp.zeros((2, 8, 128), i32)
    code2[:, :, 256:WIDE] = jnp.full((2, 8, 128), 4, i32)
    for lo, hi in ((0, 128), (128, 256), (256, SLOTS)):
        e = lists[0:ROWS, lo:hi]
        row = lax.broadcasted_iota(i32, e.shape, 0)
        i = jnp.where(row < LEAVES, row, row - LEAVES) + e
        valid = e >= 0
        index[:, lo:hi] = jnp.where(valid, i & 127, 0)
        code[:, lo:hi] = jnp.where(valid, jnp.where((e == LEAVES), 1, 0), 2)
        for j in range(2):
            e = jnp.broadcast_to(lists[ROWS + j : ROWS + j + 1, lo:hi], (8, hi - lo))
            place = ((e >> 1) & (BLOCK - 1)) * blocks + (e >> 4)
            index2[j, :, lo:hi] = jnp.where(e >= 0, place & 127, 0)
            code2[j, :, lo:hi] = jnp.where(e >= 0, (e & 1) * 2 + (place >> 7), 4)


def prepare_mats(mats, weights, g):
    for ti in range(GROUP):
        x = mats[g * GROUP + ti]
        hi = x.astype(bf16).astype(f32)
        cols = slice(ti * WIDE, (ti + 1) * WIDE)
        weights[g, 0:64, cols] = pad_mats(x).astype(bf16)
        weights[g, 64:128, cols] = pad_mats(x - hi).astype(bf16)


def pick_group(e0b, e1b, xs, index, code, picked, g):
    lane = lax.broadcasted_iota(i32, (16, 128), 1)
    sub = lax.broadcasted_iota(i32, (16, 128), 0)
    for bt in range(9):
        rows = slice(bt * 16, bt * 16 + 16)
        sources = []
        for ti in range(GROUP):
            t = g * GROUP + ti
            if bt < 8:
                own = e0b[t, :, 0:128]
                far = e0b[t, :, 128:256]
                both = [jnp.where(lane[0:8] >= sub[0:8] + (bt * 16 + h * 8), own, far) for h in range(2)]
            else:
                both = [e1b[t], e1b[t]]
            sources.append(jnp.concatenate(both, 0))
        for kt in range(3):
            i = index[rows, kt * 128 : kt * 128 + 128]
            k = code[rows, kt * 128 : kt * 128 + 128]
            for ti in range(GROUP):
                x = take(sources[ti], i)
                if bt < 8:
                    last = xs[rows, ti * 128 : ti * 128 + 128]
                    x = jnp.where(k == 0, x, jnp.where(k == 1, last, 0.0))
                else:
                    x = jnp.where(k == 0, x, 0.0)
                hi, lo = split(x)
                cols = slice(ti * WIDE + kt * 128, ti * WIDE + kt * 128 + 128)
                picked[bt * 16 : bt * 16 + 16, cols] = hi
                picked[ROWS + bt * 16 : ROWS + bt * 16 + 16, cols] = lo


def spread_group(ends, xs, g):
    row = lax.broadcasted_iota(i32, (256, GROUP * 128), 0) & 127
    col = lax.broadcasted_iota(i32, (256, GROUP * 128), 1) >> 7
    select = jnp.where(row == col + g * GROUP, 1.0, 0.0).astype(bf16)
    xs[...] = jnp.dot(ends, select, preferred_element_type=f32)


def dot_group(picked, weights, g):
    return lax.dot_general(picked[...], weights[g], (((1,), (1,)), ((), ())), preferred_element_type=f32)


def kernel(
    shape,
    field_in, contrast_in, incident_in, near_lists_in, lists_in, near_mats_in, far_mats, up_in, down_in, map_in, local_in,
    out,
    field, contrast, incident, near_lists, lists, near_mats, up, down, moment_map, local_t,
    mats, weights, picked_a, picked_b, xs_a, xs_b, index, code, index2, code2, total,
    rolled, halves, up_cat, down_cat, down_parts, m0_own, m0_ext, m1_own, m2_own, mine, tops,
    e0, e0b, e1b, near_all, p2, x2, x1,
    in_sem, mat_sem, send, recv, send1, recv1, send2, recv2, own_sem,
):
    n_owner = shape[1]
    n = shape[0] * n_owner
    blocks = n // BLOCK
    rank = lax.axis_index("group") * n_owner + lax.axis_index("owner")
    slot, block = rank % BLOCK, rank // BLOCK
    has_left, has_right = rank > 0, rank < n - 1

    def at(r):
        return (r // n_owner, r % n_owner)

    def near_peer(d):
        return block * BLOCK + (slot + d) % BLOCK

    def line_peer(d):
        return (rank + d * BLOCK) % n

    pairs = (
        (field_in, field), (contrast_in, contrast), (map_in, moment_map), (up_in, up), (lists_in, lists),
        (near_mats_in, near_mats), (near_lists_in, near_lists), (incident_in, incident), (down_in, down),
        (local_in, local_t))
    loads = [pltpu.make_async_copy(a, b, in_sem.at[i]) for i, (a, b) in enumerate(pairs)]
    for load in loads[:4]:
        load.start()
    if n < 256:
        tops[...] = jnp.zeros_like(tops)

    @pl.when(rank == 0)
    def _():
        halves[0] = jnp.zeros((64, LEAVES), f32)

    @pl.when(rank == n - 1)
    def _():
        halves[1] = jnp.zeros((64, LEAVES), f32)

    barrier = pltpu.get_barrier_semaphore()

    @pl.when(has_left)
    def _():
        pl.semaphore_signal(barrier, inc=1, device_id=at(rank - 1), device_id_type=MESH)

    @pl.when(has_right)
    def _():
        pl.semaphore_signal(barrier, inc=1, device_id=at(rank + 1), device_id_type=MESH)

    def greet_line(d, _):
        pl.semaphore_signal(barrier, inc=1, device_id=at(line_peer(d)), device_id_type=MESH)
        return 0

    def greet_near(d, _):
        pl.semaphore_signal(barrier, inc=1, device_id=at(near_peer(d)), device_id_type=MESH)
        return 0

    lax.fori_loop(1, blocks, greet_line, 0)
    lax.fori_loop(1, BLOCK, greet_near, 0)

    def start_mats(t, _):
        pltpu.make_async_copy(far_mats.at[:, t, :], mats.at[t], mat_sem.at[t]).start()
        return 0

    def wait_mats(t, _):
        pltpu.make_async_copy(far_mats.at[:, t, :], mats.at[t], mat_sem.at[t]).wait()
        return 0

    for load in loads[4:]:
        load.start()
    lax.fori_loop(0, TERMS, start_mats, 0)
    for ref in (up_cat, down_cat, m0_own, m0_ext, m1_own, m2_own, x2, x1, e1b, total):
        ref[...] = jnp.zeros_like(ref)

    for load in loads[:4]:
        load.wait()
    source = contrast[...] * field[...]
    rolled[...] = pltpu.roll(source, 64, 1)
    for c in range(8):
        up_cat[:, c * 128 : c * 128 + TERMS] = up[:, c, :]
    m0_own[:, 0:TERMS] = nt(source.T, moment_map[...])
    m1_own[:, 0:TERMS] = nt(rows_of_children(m0_own, 16), up_cat[...])
    m2_own[0:2, 0:TERMS] = nt(rows_of_children(m1_own, 2), up_cat[...])
    mine[...] = m2_own[0:1, :] + pltpu.roll(m2_own[1:2, :], 64, 1)
    own_copy = pltpu.make_async_copy(mine, tops.at[pl.ds(slot * blocks + block, 1), :], own_sem)
    own_copy.start()

    def halo(side, target):
        return pltpu.make_async_remote_copy(
            src_ref=rolled, dst_ref=halves.at[side], send_sem=send.at[side], recv_sem=recv.at[side],
            device_id=at(target), device_id_type=MESH)

    def first(d, sender):
        return pltpu.make_async_remote_copy(
            src_ref=mine, dst_ref=tops.at[pl.ds(slot * blocks + sender // BLOCK, 1), :],
            send_sem=send1.at[d], recv_sem=recv1.at[d], device_id=at(line_peer(d)), device_id_type=MESH)

    def second(d, owner):
        part = tops.at[pl.ds(owner % BLOCK * blocks, blocks), :]
        return pltpu.make_async_remote_copy(
            src_ref=part, dst_ref=part,
            send_sem=send2.at[d], recv_sem=recv2.at[d], device_id=at(near_peer(d)), device_id_type=MESH)

    def send_all():
        others = (BLOCK - 1) + (blocks - 1)
        inside = jnp.logical_and(has_left, has_right)

        @pl.when(inside)
        def _():
            pl.semaphore_wait(barrier, others + 2)

        @pl.when(jnp.logical_not(inside))
        def _():
            pl.semaphore_wait(barrier, others + 1)

        @pl.when(has_right)
        def _():
            halo(0, rank + 1).start()

        @pl.when(has_left)
        def _():
            halo(1, rank - 1).start()

        lax.fori_loop(1, blocks, lambda d, _: (first(d, rank).start(), 0)[1], 0)

    @pl.when(rank >= n // 2)
    def _():
        send_all()

    for load in loads[4:]:
        load.wait()
    for c in range(8):
        down_cat[:, c * 128 : c * 128 + TERMS] = down[:, c, :]
    d_hi = down_cat[...].astype(bf16).astype(f32)
    rest = jnp.zeros((64 - TERMS, 1024), f32)
    down_parts[...] = jnp.concatenate([d_hi, rest, down_cat[...] - d_hi, rest], 0).astype(bf16)
    prepare_lists(lists, index, code, index2, code2, blocks)
    lax.fori_loop(0, TERMS, wait_mats, 0)
    lax.fori_loop(0, NGROUP, lambda g, _: (prepare_mats(mats, weights, g), 0)[1], 0)

    @pl.when(rank < n // 2)
    def _():
        send_all()

    @pl.when(has_right)
    def _():
        halo(0, rank + 1).wait_send()

    @pl.when(has_left)
    def _():
        halo(1, rank - 1).wait_send()

    @pl.when(has_left)
    def _():
        halo(0, rank).wait_recv()

    @pl.when(has_right)
    def _():
        halo(1, rank).wait_recv()

    lane = lax.broadcasted_iota(i32, (64, 128), 1)
    ext = jnp.concatenate(
        [jnp.where(lane < 64, halves[0], rolled[...]), jnp.where(lane < 64, rolled[...], halves[1])], 1)
    e0[...] = jnp.dot(moment_map[...], ext, precision=HIGHEST, preferred_element_type=f32)
    for t in range(TERMS):
        e0b[t] = jnp.broadcast_to(e0[t : t + 1, :], (8, 256))
    m0_ext[0:128, 0:TERMS] = e0[:, 0:128].T
    m0_ext[128:256, 0:TERMS] = e0[:, 128:256].T
    e1 = nt(up_cat[...], rows_of_children(m0_ext, 32))
    for t in range(TERMS):
        e1b[t, :, 0:32] = jnp.broadcast_to(e1[t : t + 1, :], (8, 32))
    ends = jnp.concatenate(split(m0_ext[128:256, :]), 1)

    s_hi, s_lo = split(ext)
    n_hi, n_lo = split(near_mats[...].reshape(27 * 64, 64))
    near_all[...] = jnp.dot(
        jnp.concatenate([n_hi, n_hi, n_lo], 1), jnp.concatenate([s_hi, s_lo, s_hi], 0), preferred_element_type=f32)
    near = incident[...]
    for k in range(27):
        e = jnp.broadcast_to(near_lists[k : k + 1, :], (64, 128))
        i = e + lane
        valid = e >= 0
        m = jnp.where(valid, i & 127, 0)
        rows = slice(k * 64, k * 64 + 64)
        near = near + jnp.where(
            valid, jnp.where(i < 128, take(near_all[rows, 0:128], m), take(near_all[rows, 128:256], m)), 0.0)
    out[...] = near

    spread_group(ends, xs_a, 0)
    pick_group(e0b, e1b, xs_a, index, code, picked_a, 0)

    def far_pair(h, _):
        spread_group(ends, xs_b, 2 * h + 1)
        part = dot_group(picked_a, weights, 2 * h)
        pick_group(e0b, e1b, xs_b, index, code, picked_b, 2 * h + 1)
        total[...] += part
        spread_group(ends, xs_a, 2 * h + 2)
        part = dot_group(picked_b, weights, 2 * h + 1)
        pick_group(e0b, e1b, xs_a, index, code, picked_a, 2 * h + 2)
        total[...] += part
        return 0

    lax.fori_loop(0, FIRST_PAIRS, far_pair, 0)

    own_copy.wait()
    lax.fori_loop(1, blocks, lambda d, _: (first(d, (rank + n - d * BLOCK) % n).wait_recv(), 0)[1], 0)
    lax.fori_loop(1, BLOCK, lambda d, _: (second(d, rank).start(), 0)[1], 0)

    lax.fori_loop(FIRST_PAIRS, NGROUP // 2, far_pair, 0)
    total[...] += dot_group(picked_a, weights, NGROUP - 1)
    both = total[0:ROWS, :] + total[ROWS : 2 * ROWS, :]
    terms = both + pltpu.roll(both, 64, 1)

    lax.fori_loop(1, blocks, lambda d, _: (first(d, rank).wait_send(), 0)[1], 0)
    lax.fori_loop(1, BLOCK, lambda d, _: (second(d, rank).wait_send(), 0)[1], 0)
    lax.fori_loop(
        1, BLOCK, lambda d, _: (second(d, block * BLOCK + (slot + BLOCK - d) % BLOCK).wait_recv(), 0)[1], 0)
    every = tops[...].T
    for j in range(2):
        for kt in range(3):
            cols = slice(kt * 128, kt * 128 + 128)
            i = jnp.concatenate([index2[j, :, cols]] * 7, 0)
            k = jnp.concatenate([code2[j, :, cols]] * 7, 0)
            x = jnp.zeros((56, 128), f32)
            for q in range(4):
                part = every[(q >> 1) * 64 : (q >> 1) * 64 + 56, (q & 1) * 128 : (q & 1) * 128 + 128]
                x = jnp.where(k == q, take(part, i), x)
            p2[j, :, cols] = x

    sums = [jnp.zeros((TERMS, 128), f32)] * 2 + [jnp.zeros((TERMS, SLOTS - 256), f32)] * 2
    for t in range(TERMS):
        a, b, c = mats[t, :, 0:128], mats[t, :, 128:256], mats[t, :, 256:SLOTS]
        for j in range(2):
            sums[j] = sums[j] + (a * p2[j, t : t + 1, 0:128] + b * p2[j, t : t + 1, 128:256])
            sums[2 + j] = sums[2 + j] + c * p2[j, t : t + 1, 256:SLOTS]
    for j in range(2):
        x2[j * 8 : j * 8 + 8, 0:TERMS] = nt(jnp.ones((8, 128), f32), sums[j]) + nt(
            jnp.ones((8, SLOTS - 256), f32), sums[2 + j])

    def children(parents, count):
        sub = lax.broadcasted_iota(i32, (count, 128), 0) & 7
        spread = jnp.concatenate([jnp.where(sub == c, parents, 0.0) for c in range(8)], 1)
        return nt3(spread, down_parts[...])[:, 0:TERMS]

    x1[:, 0:TERMS] = terms[LEAVES:ROWS, 0:TERMS] + children(x2[...], 16)
    parents = jnp.concatenate([jnp.broadcast_to(x1[j : j + 1, :], (8, 128)) for j in range(16)], 0)
    x0 = terms[0:LEAVES, 0:TERMS] + children(parents, 128)
    out[...] += nt(local_t[...].T, x0)


def body(mesh_shape, field, contrast, incident, near_lists, far_lists, near_mats, far_mats, up_mats, down_mats,
         moment_map, local_map):
    vmem = pl.BlockSpec(memory_space=pltpu.VMEM)
    n = mesh_shape[0] * mesh_shape[1]
    dma = pltpu.SemaphoreType.DMA
    call = pl.pallas_call(
        functools.partial(kernel, mesh_shape),
        out_shape=jax.ShapeDtypeStruct((64, LEAVES), f32),
        in_specs=[pl.BlockSpec(memory_space=pl.ANY)] * 11,
        out_specs=vmem,
        scratch_shapes=[
            pltpu.VMEM((64, LEAVES), f32),
            pltpu.VMEM((64, LEAVES), f32),
            pltpu.VMEM((64, LEAVES), f32),
            pltpu.VMEM((27, LEAVES), i32),
            pltpu.VMEM((ROWS + 2, SLOTS), i32),
            pltpu.VMEM((27, 64, 64), f32),
            pltpu.VMEM((TERMS, 8, TERMS), f32),
            pltpu.VMEM((TERMS, 8, TERMS), f32),
            pltpu.VMEM((TERMS, 64), f32),
            pltpu.VMEM((TERMS, 64), f32),
            pltpu.VMEM((TERMS, TERMS, SLOTS), f32),
            pltpu.VMEM((NGROUP, 128, GROUP * WIDE), bf16),
            pltpu.VMEM((2 * ROWS, GROUP * WIDE), bf16),
            pltpu.VMEM((2 * ROWS, GROUP * WIDE), bf16),
            pltpu.VMEM((LEAVES, GROUP * 128), f32),
            pltpu.VMEM((LEAVES, GROUP * 128), f32),
            pltpu.VMEM((ROWS, WIDE), i32),
            pltpu.VMEM((ROWS, WIDE), i32),
            pltpu.VMEM((2, 8, WIDE), i32),
            pltpu.VMEM((2, 8, WIDE), i32),
            pltpu.VMEM((2 * ROWS, 128), f32),
            pltpu.VMEM((64, 128), f32),
            pltpu.VMEM((2, 64, 128), f32),
            pltpu.VMEM((TERMS, 1024), f32),
            pltpu.VMEM((TERMS, 1024), f32),
            pltpu.VMEM((128, 1024), bf16),
            pltpu.VMEM((128, 128), f32),
            pltpu.VMEM((256, 128), f32),
            pltpu.VMEM((16, 128), f32),
            pltpu.VMEM((8, 128), f32),
            pltpu.VMEM((1, 128), f32),
            pltpu.VMEM((256, 128), f32),
            pltpu.VMEM((TERMS, 256), f32),
            pltpu.VMEM((TERMS, 8, 256), f32),
            pltpu.VMEM((TERMS, 8, 128), f32),
            pltpu.VMEM((27 * 64, 256), f32),
            pltpu.VMEM((2, 56, WIDE), f32),
            pltpu.VMEM((16, 128), f32),
            pltpu.VMEM((16, 128), f32),
            dma((10,)), dma((TERMS,)), dma((2,)), dma((2,)), dma((n // BLOCK + 1,)), dma((n // BLOCK + 1,)),
            dma((BLOCK,)), dma((BLOCK,)), dma,
        ],
        compiler_params=pltpu.CompilerParams(
            collective_id=0, has_side_effects=True, vmem_limit_bytes=63 * 2**20),
    )
    return call(
        field, contrast, incident, near_lists, far_lists.T, near_mats, jnp.transpose(far_mats, (1, 2, 0)),
        jnp.transpose(up_mats, (1, 0, 2)), jnp.transpose(down_mats, (1, 0, 2)), moment_map, local_map.T)


def solution(mesh):
    line = P(None, ("group", "owner"))
    return jax.shard_map(
        functools.partial(body, (mesh.shape["group"], mesh.shape["owner"])), mesh=mesh,
        in_specs=(line,) * 5 + (P(),) * 6, out_specs=line, check_vma=False)
```
